32 devices in a mesh: grp: 2 (over y), vocab: 4 (over x, core), tile: 4 (over z).
Axes of the slice: x: 2, y: 2, z: 4, core: 2. Of those that a mesh axis runs over, the one named last changes fastest.
Arguments:
- embed: bfloat16 [512, 8192], P('vocab', 'tile'), may hold values from -6 to 6
- unembed: bfloat16 [512, 8192], P('vocab', 'tile'), may hold values from -6 to 6
- q_weight: bfloat16 [2, 8192, 4096], P(None, 'tile', 'vocab'), may hold values from -0.0625 to 0.0625
- k_weight: bfloat16 [2, 8192, 512], P(None, 'tile'), may hold values from -0.0625 to 0.0625
- v_weight: bfloat16 [2, 8192, 512], P(None, 'tile'), may hold values from -0.0625 to 0.0625
- o_weight: bfloat16 [2, 4096, 8192], P(None, 'vocab', 'tile'), may hold values from -0.0625 to 0.0625
- offsets: int32 [2], P('grp'), parts along dimension 0, may hold values from 0 to 64
Outputs:
- ov_core: float32 [4, 32, 128, 128], P('grp', 'vocab', 'tile'), parts along dimension 0
- qk_core: float32 [4, 32, 128, 128], P('grp', 'vocab', 'tile'), parts along dimension 0
The draws below stay inside these ranges and needn't reach their ends.
There are 2 independent parts, one for each index of `grp`. The reference program is written for one: setup_inputs(seed, part) draws one part's arguments, and reference() takes and returns one part's arrays. A program takes and returns all parts, laid end to end along the dimension named above; an argument that names none is the same for every part. Nothing has to cross between parts.
All inputs are finite; a program needn't handle non-finite values.
Results may differ from the reference program's by a relative error of at most 0.017.
Values may be sent and summed in bfloat16 or wider, within the bound.
A program may use at most 128 MiB of HBM per device.

```python
import math
import jax
import jax.numpy as jnp
from jax import lax

D = 8192
HD = 128
HEADS = 32
GROUP = 8
NL = 2
SLAB_DEV = 64
KVH = 4
ROWS_DEV = 128
ROWS = 512
SLAB = 256
N_VOCAB = 4
N_TILE = 4


def level_of(own_key, extent, split, low, high):
    level, own = 1.0, jax.random.fold_in(own_key, 6)
    for axis_at, parts in split:
        draws = jnp.exp(jax.random.uniform(jax.random.fold_in(own, axis_at), (parts,), jnp.float32, low / len(split), high / len(split)))
        level = level * jnp.repeat(draws, extent[axis_at] // parts).reshape([-1 if axis == axis_at else 1 for axis in range(len(extent))])
    return level


def scatter_about(stream_key, shape, spread, limit, cuts=(), kind=jnp.bfloat16):
    values = spread * jax.random.normal(stream_key, shape, jnp.float32)
    if cuts:
        values = values * level_of(stream_key, shape, cuts, -0.22, 0.18)
    return jnp.clip(values, -limit, limit).astype(kind)


def setup_inputs(seed: int = 0, part: int = 0) -> dict:
    key_of = jax.random.split(jax.random.key(seed), 8)
    own_keys = jax.random.split(jax.random.fold_in(key_of[7], part), 8)
    embed = scatter_about(key_of[0], (ROWS, D), 1.0, 6.0, ((0, 4), (1, 4)))
    unembed = scatter_about(key_of[1], (ROWS, D), 1.0, 6.0, ((0, 4), (1, 4)))
    q_weight = scatter_about(key_of[2], (NL, D, HEADS * HD), D ** -0.5, 0.0625, ((1, 4), (2, 4)))
    k_weight = scatter_about(key_of[3], (NL, D, KVH * HD), D ** -0.5, 0.0625, ((1, 4),))
    v_weight = scatter_about(key_of[4], (NL, D, KVH * HD), D ** -0.5, 0.0625, ((1, 4),))
    o_weight = scatter_about(key_of[5], (NL, HEADS * HD, D), D ** -0.5, 0.0625, ((1, 4), (2, 4)))
    offsets = jax.random.randint(own_keys[6], (1,), 0, ROWS_DEV - SLAB_DEV + 1).astype(jnp.int32)
    return {"embed": embed, "unembed": unembed, "q_weight": q_weight, "k_weight": k_weight, "v_weight": v_weight, "o_weight": o_weight, "offsets": offsets}


def width_sums(slab_rows, panel):
    block = panel.shape[0] // N_TILE
    running = jnp.zeros((slab_rows.shape[0], panel.shape[1]), jnp.float32)
    for piece_index in range(N_TILE):
        lower = piece_index * block
        product = jnp.dot(slab_rows[:, lower:lower + block], panel[lower:lower + block], preferred_element_type=jnp.float32).astype(jnp.bfloat16)
        product = lax.optimization_barrier(product)
        running = running + product.astype(jnp.float32)
    return running.astype(jnp.bfloat16)

def circuit_cores(row_side, key_side):
    rows_full = row_side.astype(jnp.float32).reshape(SLAB, KVH, GROUP, HD)
    keys_full = key_side.astype(jnp.float32).reshape(SLAB, KVH, HD)
    cores = jnp.einsum('skgr,skc->kgrc', rows_full, keys_full)
    return cores.reshape(HEADS, HD, HD) / math.sqrt(SLAB)

def take_slab(table, start_row):
    blocks = table.reshape(N_VOCAB, ROWS_DEV, D)
    return lax.dynamic_slice_in_dim(blocks, start_row, SLAB_DEV, 1).reshape(SLAB, D)

def reference(embed, unembed, q_weight, k_weight, v_weight, o_weight, offsets):
    slab_e = take_slab(embed, offsets[0])
    slab_u = take_slab(unembed, offsets[0])
    ov_list = []
    qk_list = []
    for layer_index in range(NL):
        q_side = width_sums(slab_e, q_weight[layer_index])
        k_side = width_sums(slab_e, k_weight[layer_index])
        v_side = width_sums(slab_e, v_weight[layer_index])
        o_side = width_sums(slab_u, jnp.transpose(o_weight[layer_index]))
        ov_list.append(circuit_cores(o_side, v_side))
        qk_list.append(circuit_cores(q_side, k_side))
    return (jnp.stack(ov_list), jnp.stack(qk_list))
```

```python
import math

import jax
import jax.numpy as jnp
from jax import lax
from jax.sharding import PartitionSpec as P

HD = 128
GROUP = 8
SLAB_DEV = 64


def local(embed, unembed, q_weight, k_weight, v_weight, o_weight, offsets):
    start_row = offsets[0]
    slab_e = lax.dynamic_slice_in_dim(embed, start_row, SLAB_DEV, 0)
    slab_u = lax.dynamic_slice_in_dim(unembed, start_row, SLAB_DEV, 0)
    all_e = lax.all_gather(slab_e, "vocab", axis=0, tiled=True)
    all_u = lax.all_gather(slab_u, "vocab", axis=0, tiled=True)
    layers = q_weight.shape[0]
    heads = q_weight.shape[2] // HD
    kv_start = lax.axis_index("vocab") * heads // GROUP * HD
    k_panel = lax.dynamic_slice_in_dim(k_weight, kv_start, HD, 2)
    v_panel = lax.dynamic_slice_in_dim(v_weight, kv_start, HD, 2)
    scale = 1.0 / math.sqrt(all_e.shape[0])
    tiles = lax.axis_size("tile")
    rows_each = HD // tiles
    bf16, f32 = jnp.bfloat16, jnp.float32

    k_part = jnp.einsum("sd,ldc->lsc", all_e, k_panel, preferred_element_type=f32).astype(bf16)
    v_part = jnp.einsum("sd,ldc->lsc", all_e, v_panel, preferred_element_type=f32).astype(bf16)
    k_side, v_side = lax.psum((k_part, v_part), "tile")
    k_wide = jnp.einsum("lsc,sd->lcd", k_side, all_e, preferred_element_type=f32).astype(bf16)
    v_wide = jnp.einsum("lsc,sd->lcd", v_side, all_u, preferred_element_type=f32).astype(bf16)
    qk = jnp.einsum("ldr,lcd->lrc", q_weight, k_wide, preferred_element_type=f32)
    ov = jnp.einsum("lrd,lcd->lrc", o_weight, v_wide, preferred_element_type=f32)

    def finish(part):
        part = (part * scale).astype(bf16).reshape(layers, heads, tiles, rows_each, HD)
        part = jnp.transpose(part, (2, 0, 1, 3, 4)).reshape(tiles * layers * heads * rows_each, HD)
        mine = lax.psum_scatter(part, "tile", scatter_dimension=0, tiled=True)
        return mine.reshape(layers, heads, rows_each, HD).astype(f32)

    return finish(ov), finish(qk)


def solution(mesh):
    return jax.shard_map(
        local,
        mesh=mesh,
        in_specs=(
            P("vocab", "tile"),
            P("vocab", "tile"),
            P(None, "tile", "vocab"),
            P(None, "tile", None),
            P(None, "tile", None),
            P(None, "vocab", "tile"),
            P("grp"),
        ),
        out_specs=(P("grp", "vocab", "tile", None), P("grp", "vocab", "tile", None)),
        check_vma=False,
    )
```

```python
import functools
import math

import jax
import jax.numpy as jnp
from jax import lax
from jax.experimental import pallas as pl
from jax.experimental.pallas import tpu as pltpu
from jax.sharding import PartitionSpec as P

HD = 128
GROUP = 8
SLAB_DEV = 64
MESH = pl.DeviceIdType.MESH
BF16, F32 = jnp.bfloat16, jnp.float32


def kernel(nv, nt, layers, heads, off_ref, e_hbm, u_hbm, q_hbm, k_hbm, v_hbm, o_hbm,
           ov_ref, qk_ref, e_raw, u_raw, e_all, u_all, q_w, o_w, kv_w, part, rs_in, kv_all,
           wide, c_out, c_in, raw_sem, w_sem, e_send, e_recv, u_send, u_recv,
           rs_send, rs_recv, ag_send, ag_recv, c_send, c_recv):
    vme, tme = lax.axis_index("vocab"), lax.axis_index("tile")
    v_to = [lax.rem(vme + d, nv) for d in range(nv)]
    t_to = [lax.rem(tme + d, nt) for d in range(nt)]
    t_from = [lax.rem(tme + nt - d, nt) for d in range(nt)]
    depth = e_raw.shape[1]
    rows = nv * SLAB_DEV
    chunk = rows // nt
    each = HD // nt

    barrier = pltpu.get_barrier_semaphore()
    for d in range(1, nv):
        pl.semaphore_signal(barrier, inc=1, device_id={"vocab": v_to[d]}, device_id_type=MESH)
    for d in range(1, nt):
        pl.semaphore_signal(barrier, inc=1, device_id={"tile": t_to[d]}, device_id_type=MESH)

    raw = [pltpu.make_async_copy(e_hbm, e_raw, raw_sem.at[0]),
           pltpu.make_async_copy(u_hbm, u_raw, raw_sem.at[1])]
    for copy in raw:
        copy.start()
    start = pl.multiple_of(vme * heads // GROUP * HD, HD)
    kv_loads = []
    for l in range(layers):
        for kind, src in enumerate((k_hbm, v_hbm)):
            kv_loads.append(pltpu.make_async_copy(
                src.at[l, :, pl.ds(start, HD)],
                kv_w.at[l, :, pl.ds(kind * HD, HD)], w_sem.at[2 * l + kind]))
    big_loads = []
    for kind, (src, dst) in enumerate(((q_hbm, q_w), (o_hbm, o_w))):
        for l in range(layers):
            big_loads.append(pltpu.make_async_copy(
                src.at[l], dst.at[l], w_sem.at[2 * layers + kind * layers + l]))

    off = off_ref[0]
    row = lax.broadcasted_iota(jnp.int32, (SLAB_DEV, e_raw.shape[0]), 0)
    col = lax.broadcasted_iota(jnp.int32, (SLAB_DEV, e_raw.shape[0]), 1)
    pick = jnp.where(col == row + off, 1.0, 0.0).astype(BF16)
    raw[0].wait()
    e_all[:SLAB_DEV] = jnp.dot(pick, e_raw[...], preferred_element_type=F32).astype(BF16)
    raw[1].wait()
    u_all[:SLAB_DEV] = jnp.dot(pick, u_raw[...], preferred_element_type=F32).astype(BF16)
    for copy in kv_loads + big_loads:
        copy.start()

    pl.semaphore_wait(barrier, nv - 1 + nt - 1)

    def to_vocab(buf, d, send, recv):
        return pltpu.make_async_remote_copy(
            src_ref=buf.at[pl.ds(0, SLAB_DEV)], dst_ref=buf.at[pl.ds(d * SLAB_DEV, SLAB_DEV)],
            send_sem=send.at[d], recv_sem=recv.at[d],
            device_id={"vocab": v_to[d]}, device_id_type=MESH)

    e_copies = [to_vocab(e_all, d, e_send, e_recv) for d in range(1, nv)]
    u_copies = [to_vocab(u_all, d, u_send, u_recv) for d in range(1, nv)]
    for copy in e_copies:
        copy.start()
    for copy in u_copies:
        copy.start()

    for copy in kv_loads:
        copy.wait()
    for copy in e_copies:
        copy.wait_recv()
    for l in range(layers):
        got = jnp.dot(e_all[...], kv_w[l], preferred_element_type=F32).astype(BF16)
        for t in range(nt):
            part[t, :, 2 * HD * l:2 * HD * (l + 1)] = got[t * chunk:(t + 1) * chunk]

    rs_copies = [pltpu.make_async_remote_copy(
        src_ref=part.at[t_to[d]], dst_ref=rs_in.at[d], send_sem=rs_send.at[d],
        recv_sem=rs_recv.at[d], device_id={"tile": t_to[d]}, device_id_type=MESH)
        for d in range(1, nt)]
    for copy in rs_copies:
        copy.start()
    total = part[tme].astype(F32)
    for d in range(1, nt):
        rs_copies[d - 1].wait_recv()
        total += rs_in[d].astype(F32)
    kv_all[tme] = total.astype(BF16)

    ag_copies = [pltpu.make_async_remote_copy(
        src_ref=kv_all.at[tme], dst_ref=kv_all.at[tme], send_sem=ag_send.at[d],
        recv_sem=ag_recv.at[d], device_id={"tile": t_to[d]}, device_id_type=MESH)
        for d in range(1, nt)]
    for copy in ag_copies:
        copy.start()
    for d in range(1, nt):
        pltpu.make_async_remote_copy(
            src_ref=kv_all.at[t_from[d]], dst_ref=kv_all.at[t_from[d]], send_sem=ag_send.at[d],
            recv_sem=ag_recv.at[d], device_id={"tile": t_to[d]}, device_id_type=MESH).wait_recv()

    step = min(2 * HD, heads * HD)
    pair = step // HD
    c_copies = []
    for kind in range(2):
        slab = e_all if kind == 0 else u_all
        if kind == 1:
            for copy in u_copies:
                copy.wait_recv()
        for l in range(layers):
            unit = kind * layers + l
            lane = 2 * HD * l + kind * HD
            side = kv_all[:, :, lane:lane + HD].reshape(rows, HD)
            wide[...] = lax.dot_general(side, slab[...], (((0,), (0,)), ((), ())),
                                        preferred_element_type=F32).astype(BF16)
            big_loads[unit].wait()

            def body(j, _):
                at = pl.ds(pl.multiple_of(j * step, step), step)
                if kind == 0:
                    core = jnp.dot(wide[...], q_w[l, :, at], preferred_element_type=F32).T
                else:
                    core = lax.dot_general(o_w[l, at, :], wide[...], (((1,), (1,)), ((), ())),
                                           preferred_element_type=F32)
                core = core.reshape(pair, nt, each, HD)
                to = pl.ds(pl.multiple_of(j * pair * each, pair * each), pair * each)
                for t in range(nt):
                    c_out[unit, t, to, :] = core[:, t].reshape(pair * each, HD).astype(BF16)
                return 0

            lax.fori_loop(0, heads // pair, body, 0)
            for d in range(1, nt):
                copy = pltpu.make_async_remote_copy(
                    src_ref=c_out.at[unit, t_to[d]], dst_ref=c_in.at[unit, d],
                    send_sem=c_send.at[unit, d], recv_sem=c_recv.at[unit, d],
                    device_id={"tile": t_to[d]}, device_id_type=MESH)
                copy.start()
                c_copies.append(copy)

    scale = 1.0 / math.sqrt(rows)
    for kind, out in enumerate((qk_ref, ov_ref)):
        for l in range(layers):
            unit = kind * layers + l
            total = c_out[unit, tme].astype(F32)
            for d in range(1, nt):
                c_copies[unit * (nt - 1) + d - 1].wait_recv()
                total += c_in[unit, d].astype(F32)
            out[l] = (total * scale).reshape(heads, each, HD)
    for copy in e_copies + u_copies + rs_copies + ag_copies + c_copies:
        copy.wait_send()


def local(nv, nt, embed, unembed, q_weight, k_weight, v_weight, o_weight, offsets):
    layers, depth, width = q_weight.shape
    heads, rows, each = width // HD, nv * SLAB_DEV, HD // nt
    chunk, units = rows // nt, 2 * layers
    out = jax.ShapeDtypeStruct((layers, heads, each, HD), F32)
    anywhere = pl.BlockSpec(memory_space=pl.ANY)
    vmem, dma = pltpu.VMEM, pltpu.SemaphoreType.DMA
    return pl.pallas_call(
        functools.partial(kernel, nv, nt, layers, heads),
        out_shape=(out, out),
        in_specs=[pl.BlockSpec(memory_space=pltpu.SMEM)] + [anywhere] * 6,
        out_specs=(pl.BlockSpec(memory_space=pltpu.VMEM),) * 2,
        scratch_shapes=[
            vmem(embed.shape, BF16), vmem(embed.shape, BF16),
            vmem((rows, depth), BF16), vmem((rows, depth), BF16),
            vmem((layers, depth, width), BF16), vmem((layers, width, depth), BF16),
            vmem((layers, depth, 2 * HD), BF16),
            vmem((nt, chunk, 2 * HD * layers), BF16), vmem((nt, chunk, 2 * HD * layers), BF16),
            vmem((nt, chunk, 2 * HD * layers), BF16),
            vmem((HD, depth), BF16),
            vmem((units, nt, heads * each, HD), BF16), vmem((units, nt, heads * each, HD), BF16),
            dma((2,)), dma((4 * layers,)), dma((nv,)), dma((nv,)), dma((nv,)), dma((nv,)),
            dma((nt,)), dma((nt,)), dma((nt,)), dma((nt,)), dma((units, nt)), dma((units, nt)),
        ],
        compiler_params=pltpu.CompilerParams(
            collective_id=0, has_side_effects=True, vmem_limit_bytes=61 * 2**20),
    )(offsets, embed, unembed, q_weight, k_weight, v_weight, o_weight)


def solution(mesh):
    return jax.shard_map(
        functools.partial(local, mesh.shape["vocab"], mesh.shape["tile"]),
        mesh=mesh,
        in_specs=(
            P("vocab", "tile"),
            P("vocab", "tile"),
            P(None, "tile", "vocab"),
            P(None, "tile", None),
            P(None, "tile", None),
            P(None, "vocab", "tile"),
            P("grp"),
        ),
        out_specs=(P("grp", "vocab", "tile", None), P("grp", "vocab", "tile", None)),
        check_vma=False,
    )
```

```python
import functools
import math

import jax
import jax.numpy as jnp
from jax import lax
from jax.experimental import pallas as pl
from jax.experimental.pallas import tpu as pltpu
from jax.sharding import PartitionSpec as P

HD = 128
GROUP = 8
SLAB_DEV = 64
MESH = pl.DeviceIdType.MESH
BF16, F32 = jnp.bfloat16, jnp.float32


def kernel(nv, nt, layers, heads, off_ref, e_hbm, u_hbm, q_hbm, k_hbm, v_hbm, o_hbm,
           ov_ref, qk_ref, e_raw, u_raw, e_all, u_all, q_w, o_w, kv_w, part, rs_in, kv_all,
           wide, c_out, c_mid, c_sum, c_in, raw_sem, w_sem, e_send, e_recv, u_send, u_recv,
           rs_send, rs_recv, ag_send, ag_recv, m_send, m_recv, c_send, c_recv):
    vme, tme = lax.axis_index("vocab"), lax.axis_index("tile")
    chips, half = nv // 2, nt // 2
    core = lax.rem(vme, 2)
    sibling = vme + 1 - 2 * core
    chip_to = [lax.rem(vme + 2 * d, nv) for d in range(chips)]
    parity, place = lax.rem(tme, 2), tme // 2
    other = 1 - parity
    mate = tme + 1 - 2 * parity
    place_to = [lax.rem(place + d, half) for d in range(half)]
    t_to = [lax.rem(tme + d, nt) for d in range(nt)]
    t_from = [lax.rem(tme + nt - d, nt) for d in range(nt)]
    depth = e_raw.shape[1]
    rows = nv * SLAB_DEV
    chunk = rows // nt
    each = HD // nt

    barrier = pltpu.get_barrier_semaphore()
    for v in [sibling] + chip_to[1:]:
        pl.semaphore_signal(barrier, inc=1, device_id={"vocab": v}, device_id_type=MESH)
    for d in range(1, nt):
        pl.semaphore_signal(barrier, inc=1, device_id={"tile": t_to[d]}, device_id_type=MESH)

    raw = [pltpu.make_async_copy(e_hbm, e_raw, raw_sem.at[0]),
           pltpu.make_async_copy(u_hbm, u_raw, raw_sem.at[1])]
    for copy in raw:
        copy.start()
    start = pl.multiple_of(vme * heads // GROUP * HD, HD)
    kv_loads = []
    for l in range(layers):
        for kind, src in enumerate((k_hbm, v_hbm)):
            kv_loads.append(pltpu.make_async_copy(
                src.at[l, :, pl.ds(start, HD)],
                kv_w.at[l, :, pl.ds(kind * HD, HD)], w_sem.at[2 * l + kind]))
    big_loads = []
    for kind, (src, dst) in enumerate(((q_hbm, q_w), (o_hbm, o_w))):
        for l in range(layers):
            big_loads.append(pltpu.make_async_copy(
                src.at[l], dst.at[l], w_sem.at[2 * layers + kind * layers + l]))

    off = off_ref[0]
    row = lax.broadcasted_iota(jnp.int32, (SLAB_DEV, e_raw.shape[0]), 0)
    col = lax.broadcasted_iota(jnp.int32, (SLAB_DEV, e_raw.shape[0]), 1)
    pick = jnp.where(col == row + off, 1.0, 0.0).astype(BF16)
    raw[0].wait()
    e_all[:SLAB_DEV] = jnp.dot(pick, e_raw[...], preferred_element_type=F32).astype(BF16)
    raw[1].wait()
    u_all[:SLAB_DEV] = jnp.dot(pick, u_raw[...], preferred_element_type=F32).astype(BF16)
    for copy in kv_loads + big_loads:
        copy.start()

    pl.semaphore_wait(barrier, chips + nt - 1)

    def to_vocab(buf, src, dst, v, send, recv):
        return pltpu.make_async_remote_copy(
            src_ref=buf.at[pl.ds(src * SLAB_DEV, SLAB_DEV)],
            dst_ref=buf.at[pl.ds(dst * SLAB_DEV, SLAB_DEV)],
            send_sem=send.at[dst], recv_sem=recv.at[dst],
            device_id={"vocab": v}, device_id_type=MESH)

    def gather(buf, send, recv):
        across = [to_vocab(buf, 0, 2 * d, chip_to[d], send, recv) for d in range(1, chips)]
        beside = [to_vocab(buf, 2 * d, 2 * d + 1, sibling, send, recv) for d in range(chips)]
        return across, beside

    def forward(across, beside):
        for d in range(1, chips):
            across[d - 1].wait_recv()
            beside[d].start()

    e_across, e_beside = gather(e_all, e_send, e_recv)
    u_across, u_beside = gather(u_all, u_send, u_recv)
    for copy in e_across + e_beside[:1] + u_across + u_beside[:1]:
        copy.start()

    for copy in kv_loads:
        copy.wait()
    forward(e_across, e_beside)
    for copy in e_beside:
        copy.wait_recv()

    rs_copies, ag_copies = [], []
    for kind in range(2):
        for l in range(layers):
            got = jnp.dot(e_all[...], kv_w[l, :, kind * HD:(kind + 1) * HD],
                          preferred_element_type=F32).astype(BF16)
            for t in range(nt):
                part[kind, t, :, HD * l:HD * (l + 1)] = got[t * chunk:(t + 1) * chunk]
        rs_copies.append([pltpu.make_async_remote_copy(
            src_ref=part.at[kind, t_to[d]], dst_ref=rs_in.at[kind, d],
            send_sem=rs_send.at[kind, d], recv_sem=rs_recv.at[kind, d],
            device_id={"tile": t_to[d]}, device_id_type=MESH) for d in range(1, nt)])
        for copy in rs_copies[kind]:
            copy.start()
    for kind in range(2):
        total = part[kind, tme].astype(F32)
        for d in range(1, nt):
            rs_copies[kind][d - 1].wait_recv()
            total += rs_in[kind, d].astype(F32)
        kv_all[kind, tme] = total.astype(BF16)
        ag_copies.append([pltpu.make_async_remote_copy(
            src_ref=kv_all.at[kind, tme], dst_ref=kv_all.at[kind, tme],
            send_sem=ag_send.at[kind, d], recv_sem=ag_recv.at[kind, d],
            device_id={"tile": t_to[d]}, device_id_type=MESH) for d in range(1, nt)])
        for copy in ag_copies[kind]:
            copy.start()
    forward(u_across, u_beside)

    step = min(2 * HD, heads * HD)
    pair = step // HD
    m_copies, c_copies = [], []

    def second(unit):
        m_copies[unit].wait_recv()
        copies = []
        for d in range(1, half):
            k = place_to[d]
            c_sum[unit, d] = (c_out[unit, parity, k].astype(F32)
                              + c_mid[unit, k].astype(F32)).astype(BF16)
            copies.append(pltpu.make_async_remote_copy(
                src_ref=c_sum.at[unit, d], dst_ref=c_in.at[unit, d],
                send_sem=c_send.at[unit, d], recv_sem=c_recv.at[unit, d],
                device_id={"tile": 2 * k + parity}, device_id_type=MESH))
            copies[-1].start()
        c_copies.append(copies)

    for kind in range(2):
        slab = e_all if kind == 0 else u_all
        for d in range(1, nt):
            at = kv_all.at[kind, t_from[d]]
            pltpu.make_async_remote_copy(
                src_ref=at, dst_ref=at, send_sem=ag_send.at[kind, d],
                recv_sem=ag_recv.at[kind, d], device_id={"tile": t_to[d]},
                device_id_type=MESH).wait_recv()
        if kind == 1:
            for copy in u_beside:
                copy.wait_recv()
        for l in range(layers):
            unit = kind * layers + l
            side = kv_all[kind, :, :, HD * l:HD * (l + 1)].reshape(rows, HD)
            wide[...] = lax.dot_general(side, slab[...], (((0,), (0,)), ((), ())),
                                        preferred_element_type=F32).astype(BF16)
            big_loads[unit].wait()

            def body(j, _):
                at = pl.ds(pl.multiple_of(j * step, step), step)
                if kind == 0:
                    cores = jnp.dot(wide[...], q_w[l, :, at], preferred_element_type=F32).T
                else:
                    cores = lax.dot_general(o_w[l, at, :], wide[...], (((1,), (1,)), ((), ())),
                                            preferred_element_type=F32)
                cores = cores.reshape(pair, nt, each, HD)
                to = pl.ds(pl.multiple_of(j * pair * each, pair * each), pair * each)
                for t in range(nt):
                    c_out[unit, t % 2, t // 2, to, :] = cores[:, t].reshape(pair * each, HD).astype(BF16)
                return 0

            lax.fori_loop(0, heads // pair, body, 0)
            m_copies.append(pltpu.make_async_remote_copy(
                src_ref=c_out.at[unit, other], dst_ref=c_mid.at[unit],
                send_sem=m_send.at[unit], recv_sem=m_recv.at[unit],
                device_id={"tile": mate}, device_id_type=MESH))
            m_copies[unit].start()
            if unit > 0:
                second(unit - 1)
    second(2 * layers - 1)

    scale = 1.0 / math.sqrt(rows)
    for kind, out in enumerate((qk_ref, ov_ref)):
        for l in range(layers):
            unit = kind * layers + l
            total = c_out[unit, parity, place].astype(F32) + c_mid[unit, place].astype(F32)
            for d in range(1, half):
                c_copies[unit][d - 1].wait_recv()
                total += c_in[unit, d].astype(F32)
            out[l] = (total * scale).reshape(heads, each, HD)
    for copies in [e_across, e_beside, u_across, u_beside, m_copies] + rs_copies + ag_copies + c_copies:
        for copy in copies:
            copy.wait_send()


def local(nv, nt, embed, unembed, q_weight, k_weight, v_weight, o_weight, offsets):
    layers, depth, width = q_weight.shape
    heads, rows, each = width // HD, nv * SLAB_DEV, HD // nt
    chunk, units = rows // nt, 2 * layers
    out = jax.ShapeDtypeStruct((layers, heads, each, HD), F32)
    anywhere = pl.BlockSpec(memory_space=pl.ANY)
    vmem, dma = pltpu.VMEM, pltpu.SemaphoreType.DMA
    return pl.pallas_call(
        functools.partial(kernel, nv, nt, layers, heads),
        out_shape=(out, out),
        in_specs=[pl.BlockSpec(memory_space=pltpu.SMEM)] + [anywhere] * 6,
        out_specs=(pl.BlockSpec(memory_space=pltpu.VMEM),) * 2,
        scratch_shapes=[
            vmem(embed.shape, BF16), vmem(embed.shape, BF16),
            vmem((rows, depth), BF16), vmem((rows, depth), BF16),
            vmem((layers, depth, width), BF16), vmem((layers, width, depth), BF16),
            vmem((layers, depth, 2 * HD), BF16),
            vmem((2, nt, chunk, HD * layers), BF16), vmem((2, nt, chunk, HD * layers), BF16),
            vmem((2, nt, chunk, HD * layers), BF16),
            vmem((HD, depth), BF16),
            vmem((units, 2, nt // 2, heads * each, HD), BF16),
            vmem((units, nt // 2, heads * each, HD), BF16),
            vmem((units, nt // 2, heads * each, HD), BF16),
            vmem((units, nt // 2, heads * each, HD), BF16),
            dma((2,)), dma((4 * layers,)), dma((nv,)), dma((nv,)), dma((nv,)), dma((nv,)),
            dma((2, nt)), dma((2, nt)), dma((2, nt)), dma((2, nt)),
            dma((units,)), dma((units,)), dma((units, nt // 2)), dma((units, nt // 2)),
        ],
        compiler_params=pltpu.CompilerParams(
            collective_id=0, has_side_effects=True, vmem_limit_bytes=61 * 2**20),
    )(offsets, embed, unembed, q_weight, k_weight, v_weight, o_weight)


def solution(mesh):
    return jax.shard_map(
        functools.partial(local, mesh.shape["vocab"], mesh.shape["tile"]),
        mesh=mesh,
        in_specs=(
            P("vocab", "tile"),
            P("vocab", "tile"),
            P(None, "tile", "vocab"),
            P(None, "tile", None),
            P(None, "tile", None),
            P(None, "vocab", "tile"),
            P("grp"),
        ),
        out_specs=(P("grp", "vocab", "tile", None), P("grp", "vocab", "tile", None)),
        check_vma=False,
    )
```

```python
import functools
import math

import jax
import jax.numpy as jnp
from jax import lax
from jax.experimental import pallas as pl
from jax.experimental.pallas import tpu as pltpu
from jax.sharding import PartitionSpec as P

HD = 128
GROUP = 8
SLAB_DEV = 64
MESH = pl.DeviceIdType.MESH
BF16, F32 = jnp.bfloat16, jnp.float32


def kernel(nv, nt, layers, heads, off_ref, e_hbm, u_hbm, q_hbm, k_hbm, v_hbm, o_hbm,
           out_ref, e_raw, u_raw, e_all, u_all, q_w, o_w, kv_w, part, rs_in, kv_all,
           wide, c_out, c_mid, c_sum, c_in, raw_sem, w_sem, e_send, e_recv, u_send, u_recv,
           rs_send, rs_recv, ag_send, ag_recv, m_send, m_recv, c_send, c_recv):
    vme, tme = lax.axis_index("vocab"), lax.axis_index("tile")
    chips, half = nv // 2, nt // 2
    core = lax.rem(vme, 2)
    sibling = vme + 1 - 2 * core
    chip_to = [lax.rem(vme + 2 * d, nv) for d in range(chips)]
    parity, place = lax.rem(tme, 2), tme // 2
    other = 1 - parity
    mate = tme + 1 - 2 * parity
    place_to = [lax.rem(place + d, half) for d in range(half)]
    t_to = [lax.rem(tme + d, nt) for d in range(nt)]
    t_from = [lax.rem(tme + nt - d, nt) for d in range(nt)]
    depth = e_raw.shape[1]
    rows = nv * SLAB_DEV
    chunk = rows // nt
    each = HD // nt

    barrier = pltpu.get_barrier_semaphore()
    for v in [sibling] + chip_to[1:]:
        pl.semaphore_signal(barrier, inc=1, device_id={"vocab": v}, device_id_type=MESH)
    for d in range(1, nt):
        pl.semaphore_signal(barrier, inc=1, device_id={"tile": t_to[d]}, device_id_type=MESH)

    raw = [pltpu.make_async_copy(e_hbm, e_raw, raw_sem.at[0]),
           pltpu.make_async_copy(u_hbm, u_raw, raw_sem.at[1])]
    for copy in raw:
        copy.start()
    start = pl.multiple_of(vme * heads // GROUP * HD, HD)
    kv_loads = []
    for l in range(layers):
        for kind, src in enumerate((k_hbm, v_hbm)):
            kv_loads.append(pltpu.make_async_copy(
                src.at[l, :, pl.ds(start, HD)],
                kv_w.at[l, :, pl.ds(kind * HD, HD)], w_sem.at[2 * l + kind]))
    big_loads = []
    for kind, (src, dst) in enumerate(((q_hbm, q_w), (o_hbm, o_w))):
        for l in range(layers):
            big_loads.append(pltpu.make_async_copy(
                src.at[l], dst.at[l], w_sem.at[2 * layers + kind * layers + l]))

    off = off_ref[0]
    row = lax.broadcasted_iota(jnp.int32, (SLAB_DEV, e_raw.shape[0]), 0)
    col = lax.broadcasted_iota(jnp.int32, (SLAB_DEV, e_raw.shape[0]), 1)
    pick = jnp.where(col == row + off, 1.0, 0.0).astype(BF16)
    raw[0].wait()
    e_all[:SLAB_DEV] = jnp.dot(pick, e_raw[...], preferred_element_type=F32).astype(BF16)
    raw[1].wait()
    u_all[:SLAB_DEV] = jnp.dot(pick, u_raw[...], preferred_element_type=F32).astype(BF16)
    for copy in kv_loads + big_loads:
        copy.start()

    pl.semaphore_wait(barrier, chips + nt - 1)

    def to_vocab(buf, src, dst, v, send, recv):
        return pltpu.make_async_remote_copy(
            src_ref=buf.at[pl.ds(src * SLAB_DEV, SLAB_DEV)],
            dst_ref=buf.at[pl.ds(dst * SLAB_DEV, SLAB_DEV)],
            send_sem=send.at[dst], recv_sem=recv.at[dst],
            device_id={"vocab": v}, device_id_type=MESH)

    def gather(buf, send, recv):
        across = [to_vocab(buf, 0, 2 * d, chip_to[d], send, recv) for d in range(1, chips)]
        beside = [to_vocab(buf, 2 * d, 2 * d + 1, sibling, send, recv) for d in range(chips)]
        return across, beside

    def forward(across, beside):
        for d in range(1, chips):
            across[d - 1].wait_recv()
            beside[d].start()

    e_across, e_beside = gather(e_all, e_send, e_recv)
    u_across, u_beside = gather(u_all, u_send, u_recv)
    for copy in e_across + e_beside[:1]:
        copy.start()

    for copy in kv_loads:
        copy.wait()
    forward(e_across, e_beside)
    for copy in u_across + u_beside[:1]:
        copy.start()
    for copy in e_beside:
        copy.wait_recv()

    rs_copies, ag_copies = [], []
    for kind in range(2):
        for l in range(layers):
            got = jnp.dot(e_all[...], kv_w[l, :, kind * HD:(kind + 1) * HD],
                          preferred_element_type=F32).astype(BF16)
            for t in range(nt):
                part[kind, t, :, HD * l:HD * (l + 1)] = got[t * chunk:(t + 1) * chunk]
        rs_copies.append([pltpu.make_async_remote_copy(
            src_ref=part.at[kind, t_to[d]], dst_ref=rs_in.at[kind, d],
            send_sem=rs_send.at[kind, d], recv_sem=rs_recv.at[kind, d],
            device_id={"tile": t_to[d]}, device_id_type=MESH) for d in range(1, nt)])
        for copy in rs_copies[kind]:
            copy.start()
    for kind in range(2):
        total = part[kind, tme].astype(F32)
        for d in range(1, nt):
            rs_copies[kind][d - 1].wait_recv()
            total += rs_in[kind, d].astype(F32)
        kv_all[kind, tme] = total.astype(BF16)
        ag_copies.append([pltpu.make_async_remote_copy(
            src_ref=kv_all.at[kind, tme], dst_ref=kv_all.at[kind, tme],
            send_sem=ag_send.at[kind, d], recv_sem=ag_recv.at[kind, d],
            device_id={"tile": t_to[d]}, device_id_type=MESH) for d in range(1, nt)])
        for copy in ag_copies[kind]:
            copy.start()
    forward(u_across, u_beside)

    step = min(2 * HD, heads * HD)
    pair = step // HD
    m_copies, c_copies = [], []

    def second(unit):
        m_copies[unit].wait_recv()
        copies = []
        for d in range(1, half):
            k = place_to[d]
            c_sum[unit, d] = (c_out[unit, parity, k].astype(F32)
                              + c_mid[unit, k].astype(F32)).astype(BF16)
            copies.append(pltpu.make_async_remote_copy(
                src_ref=c_sum.at[unit, d], dst_ref=c_in.at[unit, d],
                send_sem=c_send.at[unit, d], recv_sem=c_recv.at[unit, d],
                device_id={"tile": 2 * k + parity}, device_id_type=MESH))
            copies[-1].start()
        c_copies.append(copies)

    for kind in range(2):
        slab = e_all if kind == 0 else u_all
        for d in range(1, nt):
            at = kv_all.at[kind, t_from[d]]
            pltpu.make_async_remote_copy(
                src_ref=at, dst_ref=at, send_sem=ag_send.at[kind, d],
                recv_sem=ag_recv.at[kind, d], device_id={"tile": t_to[d]},
                device_id_type=MESH).wait_recv()
        if kind == 1:
            for copy in u_beside:
                copy.wait_recv()
        for l in range(layers):
            unit = kind * layers + l
            side = kv_all[kind, :, :, HD * l:HD * (l + 1)].reshape(rows, HD)
            wide[...] = lax.dot_general(side, slab[...], (((0,), (0,)), ((), ())),
                                        preferred_element_type=F32).astype(BF16)
            big_loads[unit].wait()

            def body(j, _):
                at = pl.ds(pl.multiple_of(j * step, step), step)
                if kind == 0:
                    cores = jnp.dot(wide[...], q_w[l, :, at], preferred_element_type=F32).T
                else:
                    cores = lax.dot_general(o_w[l, at, :], wide[...], (((1,), (1,)), ((), ())),
                                            preferred_element_type=F32)
                cores = cores.reshape(pair, nt, each, HD)
                to = pl.ds(pl.multiple_of(j * pair * each, pair * each), pair * each)
                for t in range(nt):
                    c_out[unit, t % 2, t // 2, to, :] = cores[:, t].reshape(pair * each, HD).astype(BF16)
                return 0

            lax.fori_loop(0, heads // pair, body, 0)
            m_copies.append(pltpu.make_async_remote_copy(
                src_ref=c_out.at[unit, other], dst_ref=c_mid.at[unit],
                send_sem=m_send.at[unit], recv_sem=m_recv.at[unit],
                device_id={"tile": mate}, device_id_type=MESH))
            m_copies[unit].start()
            if unit > 0:
                second(unit - 1)
    second(2 * layers - 1)

    for kind in range(2):
        for l in range(layers):
            unit = kind * layers + l
            total = c_out[unit, parity, place].astype(F32) + c_mid[unit, place].astype(F32)
            for d in range(1, half):
                c_copies[unit][d - 1].wait_recv()
                total += c_in[unit, d].astype(F32)
            out_ref[1 - kind, l] = total.reshape(heads, each, HD)
    for copies in [e_across, e_beside, u_across, u_beside, m_copies] + rs_copies + ag_copies + c_copies:
        for copy in copies:
            copy.wait_send()


def local(nv, nt, embed, unembed, q_weight, k_weight, v_weight, o_weight, offsets):
    layers, depth, width = q_weight.shape
    heads, rows, each = width // HD, nv * SLAB_DEV, HD // nt
    chunk, units = rows // nt, 2 * layers
    out = jax.ShapeDtypeStruct((2, layers, heads, each, HD), F32)
    anywhere = pl.BlockSpec(memory_space=pl.ANY)
    vmem, dma = pltpu.VMEM, pltpu.SemaphoreType.DMA
    cores = pl.pallas_call(
        functools.partial(kernel, nv, nt, layers, heads),
        out_shape=out,
        in_specs=[pl.BlockSpec(memory_space=pltpu.SMEM)] + [anywhere] * 6,
        out_specs=pl.BlockSpec(memory_space=pltpu.VMEM),
        scratch_shapes=[
            vmem(embed.shape, BF16), vmem(embed.shape, BF16),
            vmem((rows, depth), BF16), vmem((rows, depth), BF16),
            vmem((layers, depth, width), BF16), vmem((layers, width, depth), BF16),
            vmem((layers, depth, 2 * HD), BF16),
            vmem((2, nt, chunk, HD * layers), BF16), vmem((2, nt, chunk, HD * layers), BF16),
            vmem((2, nt, chunk, HD * layers), BF16),
            vmem((HD, depth), BF16),
            vmem((units, 2, nt // 2, heads * each, HD), BF16),
            vmem((units, nt // 2, heads * each, HD), BF16),
            vmem((units, nt // 2, heads * each, HD), BF16),
            vmem((units, nt // 2, heads * each, HD), BF16),
            dma((2,)), dma((4 * layers,)), dma((nv,)), dma((nv,)), dma((nv,)), dma((nv,)),
            dma((2, nt)), dma((2, nt)), dma((2, nt)), dma((2, nt)),
            dma((units,)), dma((units,)), dma((units, nt // 2)), dma((units, nt // 2)),
        ],
        compiler_params=pltpu.CompilerParams(
            collective_id=0, has_side_effects=True, vmem_limit_bytes=61 * 2**20),
    )(offsets, embed, unembed, q_weight, k_weight, v_weight, o_weight)
    scale = 1.0 / math.sqrt(rows)
    return cores[0] * scale, cores[1] * scale


def solution(mesh):
    return jax.shard_map(
        functools.partial(local, mesh.shape["vocab"], mesh.shape["tile"]),
        mesh=mesh,
        in_specs=(
            P("vocab", "tile"),
            P("vocab", "tile"),
            P(None, "tile", "vocab"),
            P(None, "tile", None),
            P(None, "tile", None),
            P(None, "vocab", "tile"),
            P("grp"),
        ),
        out_specs=(P("grp", "vocab", "tile", None), P("grp", "vocab", "tile", None)),
        check_vma=False,
    )
```

```python
import functools
import math

import jax
import jax.numpy as jnp
from jax import lax
from jax.experimental import pallas as pl
from jax.experimental.pallas import tpu as pltpu
from jax.sharding import PartitionSpec as P

HD = 128
GROUP = 8
SLAB_DEV = 64
MESH = pl.DeviceIdType.MESH
BF16, F32 = jnp.bfloat16, jnp.float32


def kernel(nv, nt, layers, heads, off_ref, e_hbm, u_hbm, q_hbm, k_hbm, v_hbm, o_hbm,
           out_ref, e_raw, u_raw, e_all, u_all, q_w, o_w, kv_w, part, rs_in, kv_all,
           wide, c_out, c_mid, c_sum, c_in, raw_sem, w_sem, e_send, e_recv, u_send, u_recv,
           rs_send, rs_recv, ag_send, ag_recv, m_send, m_recv, c_send, c_recv):
    vme, tme = lax.axis_index("vocab"), lax.axis_index("tile")
    chips, half = nv // 2, nt // 2
    core = lax.rem(vme, 2)
    sibling = vme + 1 - 2 * core
    chip_to = [lax.rem(vme + 2 * d, nv) for d in range(chips)]
    parity, place = lax.rem(tme, 2), tme // 2
    other = 1 - parity
    mate = tme + 1 - 2 * parity
    place_to = [lax.rem(place + d, half) for d in range(half)]
    t_to = [lax.rem(tme + d, nt) for d in range(nt)]
    t_from = [lax.rem(tme + nt - d, nt) for d in range(nt)]
    depth = e_raw.shape[1]
    rows = nv * SLAB_DEV
    chunk = rows // nt
    each = HD // nt

    barrier = pltpu.get_barrier_semaphore()
    for v in [sibling] + chip_to[1:]:
        pl.semaphore_signal(barrier, inc=1, device_id={"vocab": v}, device_id_type=MESH)
    for d in range(1, nt):
        pl.semaphore_signal(barrier, inc=1, device_id={"tile": t_to[d]}, device_id_type=MESH)

    raw = [pltpu.make_async_copy(e_hbm, e_raw, raw_sem.at[0]),
           pltpu.make_async_copy(u_hbm, u_raw, raw_sem.at[1])]
    for copy in raw:
        copy.start()
    start = pl.multiple_of(vme * heads // GROUP * HD, HD)
    kv_loads = []
    for l in range(layers):
        for kind, src in enumerate((k_hbm, v_hbm)):
            kv_loads.append(pltpu.make_async_copy(
                src.at[l, :, pl.ds(start, HD)],
                kv_w.at[l, :, pl.ds(kind * HD, HD)], w_sem.at[2 * l + kind]))
    big_loads = []
    for kind, (src, dst) in enumerate(((q_hbm, q_w), (o_hbm, o_w))):
        for l in range(layers):
            big_loads.append(pltpu.make_async_copy(
                src.at[l], dst.at[l], w_sem.at[2 * layers + kind * layers + l]))

    off = off_ref[0]
    row = lax.broadcasted_iota(jnp.int32, (SLAB_DEV, e_raw.shape[0]), 0)
    col = lax.broadcasted_iota(jnp.int32, (SLAB_DEV, e_raw.shape[0]), 1)
    pick = jnp.where(col == row + off, 1.0, 0.0).astype(BF16)
    raw[0].wait()
    e_all[:SLAB_DEV] = jnp.dot(pick, e_raw[...], preferred_element_type=F32).astype(BF16)
    raw[1].wait()
    u_all[:SLAB_DEV] = jnp.dot(pick, u_raw[...], preferred_element_type=F32).astype(BF16)
    for copy in kv_loads + big_loads:
        copy.start()

    pl.semaphore_wait(barrier, chips + nt - 1)

    def to_vocab(buf, src, dst, v, send, recv):
        return pltpu.make_async_remote_copy(
            src_ref=buf.at[pl.ds(src * SLAB_DEV, SLAB_DEV)],
            dst_ref=buf.at[pl.ds(dst * SLAB_DEV, SLAB_DEV)],
            send_sem=send.at[dst], recv_sem=recv.at[dst],
            device_id={"vocab": v}, device_id_type=MESH)

    def gather(buf, send, recv):
        across = [to_vocab(buf, 0, 2 * d, chip_to[d], send, recv) for d in range(1, chips)]
        beside = [to_vocab(buf, 2 * d, 2 * d + 1, sibling, send, recv) for d in range(chips)]
        return across, beside

    def forward(across, beside):
        for d in range(1, chips):
            across[d - 1].wait_recv()
            beside[d].start()

    e_across, e_beside = gather(e_all, e_send, e_recv)
    u_across, u_beside = gather(u_all, u_send, u_recv)
    for copy in e_across + e_beside[:1]:
        copy.start()

    for copy in kv_loads:
        copy.wait()
    forward(e_across, e_beside)
    for copy in u_across + u_beside[:1]:
        copy.start()
    for copy in e_beside:
        copy.wait_recv()

    rs_copies, ag_copies = [], []
    for kind in range(2):
        for l in range(layers):
            got = jnp.dot(e_all[...], kv_w[l, :, kind * HD:(kind + 1) * HD],
                          preferred_element_type=F32).astype(BF16)
            for t in range(nt):
                part[kind, t, :, HD * l:HD * (l + 1)] = got[t * chunk:(t + 1) * chunk]
        rs_copies.append([pltpu.make_async_remote_copy(
            src_ref=part.at[kind, t_to[d]], dst_ref=rs_in.at[kind, d],
            send_sem=rs_send.at[kind, d], recv_sem=rs_recv.at[kind, d],
            device_id={"tile": t_to[d]}, device_id_type=MESH) for d in range(1, nt)])
        for copy in rs_copies[kind]:
            copy.start()
    for kind in range(2):
        total = part[kind, tme].astype(F32)
        for d in range(1, nt):
            rs_copies[kind][d - 1].wait_recv()
            total += rs_in[kind, d].astype(F32)
        kv_all[kind, tme] = total.astype(BF16)
        ag_copies.append([pltpu.make_async_remote_copy(
            src_ref=kv_all.at[kind, tme], dst_ref=kv_all.at[kind, tme],
            send_sem=ag_send.at[kind, d], recv_sem=ag_recv.at[kind, d],
            device_id={"tile": t_to[d]}, device_id_type=MESH) for d in range(1, nt)])
        for copy in ag_copies[kind]:
            copy.start()
    forward(u_across, u_beside)

    step = min(4 * HD, heads * HD)
    pair = step // HD
    m_copies, c_copies = [], []

    def second(unit):
        m_copies[unit].wait_recv()
        copies = []
        for d in range(1, half):
            k = place_to[d]
            c_sum[unit, d] = (c_out[unit, parity, k].astype(F32)
                              + c_mid[unit, k].astype(F32)).astype(BF16)
            copies.append(pltpu.make_async_remote_copy(
                src_ref=c_sum.at[unit, d], dst_ref=c_in.at[unit, d],
                send_sem=c_send.at[unit, d], recv_sem=c_recv.at[unit, d],
                device_id={"tile": 2 * k + parity}, device_id_type=MESH))
            copies[-1].start()
        c_copies.append(copies)

    for kind in range(2):
        slab = e_all if kind == 0 else u_all
        for d in range(1, nt):
            at = kv_all.at[kind, t_from[d]]
            pltpu.make_async_remote_copy(
                src_ref=at, dst_ref=at, send_sem=ag_send.at[kind, d],
                recv_sem=ag_recv.at[kind, d], device_id={"tile": t_to[d]},
                device_id_type=MESH).wait_recv()
        if kind == 1:
            for copy in u_beside:
                copy.wait_recv()
        for l in range(layers):
            unit = kind * layers + l
            side = kv_all[kind, :, :, HD * l:HD * (l + 1)].reshape(rows, HD)
            wide[...] = lax.dot_general(side, slab[...], (((0,), (0,)), ((), ())),
                                        preferred_element_type=F32).astype(BF16)
            big_loads[unit].wait()

            def body(j, _):
                at = pl.ds(pl.multiple_of(j * step, step), step)
                if kind == 0:
                    cores = jnp.dot(wide[...], q_w[l, :, at], preferred_element_type=F32).T
                else:
                    cores = lax.dot_general(o_w[l, at, :], wide[...], (((1,), (1,)), ((), ())),
                                            preferred_element_type=F32)
                cores = cores.reshape(pair, nt, each, HD)
                to = pl.ds(pl.multiple_of(j * pair * each, pair * each), pair * each)
                for t in range(nt):
                    c_out[unit, t % 2, t // 2, to, :] = cores[:, t].reshape(pair * each, HD).astype(BF16)
                return 0

            lax.fori_loop(0, heads // pair, body, 0, unroll=True)
            m_copies.append(pltpu.make_async_remote_copy(
                src_ref=c_out.at[unit, other], dst_ref=c_mid.at[unit],
                send_sem=m_send.at[unit], recv_sem=m_recv.at[unit],
                device_id={"tile": mate}, device_id_type=MESH))
            m_copies[unit].start()
            if unit > 0:
                second(unit - 1)
    second(2 * layers - 1)

    for kind in range(2):
        for l in range(layers):
            unit = kind * layers + l
            total = c_out[unit, parity, place].astype(F32) + c_mid[unit, place].astype(F32)
            for d in range(1, half):
                c_copies[unit][d - 1].wait_recv()
                total += c_in[unit, d].astype(F32)
            out_ref[1 - kind, l] = total.reshape(heads, each, HD)
    for copies in [e_across, e_beside, u_across, u_beside, m_copies] + rs_copies + ag_copies + c_copies:
        for copy in copies:
            copy.wait_send()


def local(nv, nt, embed, unembed, q_weight, k_weight, v_weight, o_weight, offsets):
    layers, depth, width = q_weight.shape
    heads, rows, each = width // HD, nv * SLAB_DEV, HD // nt
    chunk, units = rows // nt, 2 * layers
    out = jax.ShapeDtypeStruct((2, layers, heads, each, HD), F32)
    anywhere = pl.BlockSpec(memory_space=pl.ANY)
    vmem, dma = pltpu.VMEM, pltpu.SemaphoreType.DMA
    cores = pl.pallas_call(
        functools.partial(kernel, nv, nt, layers, heads),
        out_shape=out,
        in_specs=[pl.BlockSpec(memory_space=pltpu.SMEM)] + [anywhere] * 6,
        out_specs=pl.BlockSpec(memory_space=pltpu.VMEM),
        scratch_shapes=[
            vmem(embed.shape, BF16), vmem(embed.shape, BF16),
            vmem((rows, depth), BF16), vmem((rows, depth), BF16),
            vmem((layers, depth, width), BF16), vmem((layers, width, depth), BF16),
            vmem((layers, depth, 2 * HD), BF16),
            vmem((2, nt, chunk, HD * layers), BF16), vmem((2, nt, chunk, HD * layers), BF16),
            vmem((2, nt, chunk, HD * layers), BF16),
            vmem((HD, depth), BF16),
            vmem((units, 2, nt // 2, heads * each, HD), BF16),
            vmem((units, nt // 2, heads * each, HD), BF16),
            vmem((units, nt // 2, heads * each, HD), BF16),
            vmem((units, nt // 2, heads * each, HD), BF16),
            dma((2,)), dma((4 * layers,)), dma((nv,)), dma((nv,)), dma((nv,)), dma((nv,)),
            dma((2, nt)), dma((2, nt)), dma((2, nt)), dma((2, nt)),
            dma((units,)), dma((units,)), dma((units, nt // 2)), dma((units, nt // 2)),
        ],
        compiler_params=pltpu.CompilerParams(
            collective_id=0, has_side_effects=True, vmem_limit_bytes=61 * 2**20),
    )(offsets, embed, unembed, q_weight, k_weight, v_weight, o_weight)
    scale = 1.0 / math.sqrt(rows)
    return cores[0] * scale, cores[1] * scale


def solution(mesh):
    return jax.shard_map(
        functools.partial(local, mesh.shape["vocab"], mesh.shape["tile"]),
        mesh=mesh,
        in_specs=(
            P("vocab", "tile"),
            P("vocab", "tile"),
            P(None, "tile", "vocab"),
            P(None, "tile", None),
            P(None, "tile", None),
            P(None, "vocab", "tile"),
            P("grp"),
        ),
        out_specs=(P("grp", "vocab", "tile", None), P("grp", "vocab", "tile", None)),
        check_vma=False,
    )
```

```python
import functools
import math

import jax
import jax.numpy as jnp
from jax import lax
from jax.experimental import pallas as pl
from jax.experimental.pallas import tpu as pltpu
from jax.sharding import PartitionSpec as P

HD = 128
GROUP = 8
SLAB_DEV = 64
MESH = pl.DeviceIdType.MESH
BF16, F32 = jnp.bfloat16, jnp.float32


def kernel(nv, nt, layers, heads, off_ref, e_hbm, u_hbm, q_hbm, k_hbm, v_hbm, o_hbm,
           out_ref, e_raw, u_raw, e_all, u_all, q_w, o_w, kv_w, part, rs_in, kv_all,
           wide, c_out, c_mid, c_sum, c_in, c_dir, raw_sem, w_sem, e_send, e_recv, u_send, u_recv,
           rs_send, rs_recv, ag_send, ag_recv, m_send, m_recv, c_send, c_recv,
           d_send, d_recv):
    vme, tme = lax.axis_index("vocab"), lax.axis_index("tile")
    chips, half = nv // 2, nt // 2
    core = lax.rem(vme, 2)
    sibling = vme + 1 - 2 * core
    chip_to = [lax.rem(vme + 2 * d, nv) for d in range(chips)]
    parity, place = lax.rem(tme, 2), tme // 2
    other = 1 - parity
    mate = tme + 1 - 2 * parity
    place_to = [lax.rem(place + d, half) for d in range(half)]
    t_to = [lax.rem(tme + d, nt) for d in range(nt)]
    t_from = [lax.rem(tme + nt - d, nt) for d in range(nt)]
    depth = e_raw.shape[1]
    rows = nv * SLAB_DEV
    chunk = rows // nt
    each = HD // nt

    barrier = pltpu.get_barrier_semaphore()
    for v in [sibling] + chip_to[1:]:
        pl.semaphore_signal(barrier, inc=1, device_id={"vocab": v}, device_id_type=MESH)
    for d in range(1, nt):
        pl.semaphore_signal(barrier, inc=1, device_id={"tile": t_to[d]}, device_id_type=MESH)

    raw = [pltpu.make_async_copy(e_hbm, e_raw, raw_sem.at[0]),
           pltpu.make_async_copy(u_hbm, u_raw, raw_sem.at[1])]
    for copy in raw:
        copy.start()
    start = pl.multiple_of(vme * heads // GROUP * HD, HD)
    kv_loads = []
    for l in range(layers):
        for kind, src in enumerate((k_hbm, v_hbm)):
            kv_loads.append(pltpu.make_async_copy(
                src.at[l, :, pl.ds(start, HD)],
                kv_w.at[l, :, pl.ds(kind * HD, HD)], w_sem.at[2 * l + kind]))
    big_loads = []
    for kind, (src, dst) in enumerate(((q_hbm, q_w), (o_hbm, o_w))):
        for l in range(layers):
            big_loads.append(pltpu.make_async_copy(
                src.at[l], dst.at[l], w_sem.at[2 * layers + kind * layers + l]))

    off = off_ref[0]
    row = lax.broadcasted_iota(jnp.int32, (SLAB_DEV, e_raw.shape[0]), 0)
    col = lax.broadcasted_iota(jnp.int32, (SLAB_DEV, e_raw.shape[0]), 1)
    pick = jnp.where(col == row + off, 1.0, 0.0).astype(BF16)
    raw[0].wait()
    e_all[:SLAB_DEV] = jnp.dot(pick, e_raw[...], preferred_element_type=F32).astype(BF16)
    raw[1].wait()
    u_all[:SLAB_DEV] = jnp.dot(pick, u_raw[...], preferred_element_type=F32).astype(BF16)
    for copy in kv_loads + big_loads:
        copy.start()

    pl.semaphore_wait(barrier, chips + nt - 1)

    def to_vocab(buf, src, dst, v, send, recv):
        return pltpu.make_async_remote_copy(
            src_ref=buf.at[pl.ds(src * SLAB_DEV, SLAB_DEV)],
            dst_ref=buf.at[pl.ds(dst * SLAB_DEV, SLAB_DEV)],
            send_sem=send.at[dst], recv_sem=recv.at[dst],
            device_id={"vocab": v}, device_id_type=MESH)

    def gather(buf, send, recv):
        across = [to_vocab(buf, 0, 2 * d, chip_to[d], send, recv) for d in range(1, chips)]
        beside = [to_vocab(buf, 2 * d, 2 * d + 1, sibling, send, recv) for d in range(chips)]
        return across, beside

    def forward(across, beside):
        for d in range(1, chips):
            across[d - 1].wait_recv()
            beside[d].start()

    e_across, e_beside = gather(e_all, e_send, e_recv)
    u_across, u_beside = gather(u_all, u_send, u_recv)
    for copy in e_across + e_beside[:1]:
        copy.start()

    for copy in kv_loads:
        copy.wait()
    forward(e_across, e_beside)
    for copy in u_across + u_beside[:1]:
        copy.start()
    for copy in e_beside:
        copy.wait_recv()

    rs_copies, ag_copies = [], []
    for kind in range(2):
        for l in range(layers):
            got = jnp.dot(e_all[...], kv_w[l, :, kind * HD:(kind + 1) * HD],
                          preferred_element_type=F32).astype(BF16)
            for t in range(nt):
                part[kind, t, :, HD * l:HD * (l + 1)] = got[t * chunk:(t + 1) * chunk]
        rs_copies.append([pltpu.make_async_remote_copy(
            src_ref=part.at[kind, t_to[d]], dst_ref=rs_in.at[kind, d],
            send_sem=rs_send.at[kind, d], recv_sem=rs_recv.at[kind, d],
            device_id={"tile": t_to[d]}, device_id_type=MESH) for d in range(1, nt)])
        for copy in rs_copies[kind]:
            copy.start()
    for kind in range(2):
        total = part[kind, tme].astype(F32)
        for d in range(1, nt):
            rs_copies[kind][d - 1].wait_recv()
            total += rs_in[kind, d].astype(F32)
        kv_all[kind, tme] = total.astype(BF16)
        ag_copies.append([pltpu.make_async_remote_copy(
            src_ref=kv_all.at[kind, tme], dst_ref=kv_all.at[kind, tme],
            send_sem=ag_send.at[kind, d], recv_sem=ag_recv.at[kind, d],
            device_id={"tile": t_to[d]}, device_id_type=MESH) for d in range(1, nt)])
        for copy in ag_copies[kind]:
            copy.start()
    forward(u_across, u_beside)

    step = min(2 * HD, heads * HD)
    pair = step // HD
    m_copies, c_copies, last = [], [], 2 * layers - 1

    def second(unit):
        m_copies[unit].wait_recv()
        copies = []
        for d in range(1, half):
            k = place_to[d]
            c_sum[unit, d] = (c_out[unit, parity, k].astype(F32)
                              + c_mid[unit, k].astype(F32)).astype(BF16)
            copies.append(pltpu.make_async_remote_copy(
                src_ref=c_sum.at[unit, d], dst_ref=c_in.at[unit, d],
                send_sem=c_send.at[unit, d], recv_sem=c_recv.at[unit, d],
                device_id={"tile": 2 * k + parity}, device_id_type=MESH))
            copies[-1].start()
        c_copies.append(copies)

    for kind in range(2):
        slab = e_all if kind == 0 else u_all
        for d in range(1, nt):
            at = kv_all.at[kind, t_from[d]]
            pltpu.make_async_remote_copy(
                src_ref=at, dst_ref=at, send_sem=ag_send.at[kind, d],
                recv_sem=ag_recv.at[kind, d], device_id={"tile": t_to[d]},
                device_id_type=MESH).wait_recv()
        if kind == 1:
            for copy in u_beside:
                copy.wait_recv()
        for l in range(layers):
            unit = kind * layers + l
            side = kv_all[kind, :, :, HD * l:HD * (l + 1)].reshape(rows, HD)
            wide[...] = lax.dot_general(side, slab[...], (((0,), (0,)), ((), ())),
                                        preferred_element_type=F32).astype(BF16)
            big_loads[unit].wait()

            def body(j, _):
                at = pl.ds(pl.multiple_of(j * step, step), step)
                if kind == 0:
                    cores = jnp.dot(wide[...], q_w[l, :, at], preferred_element_type=F32).T
                else:
                    cores = lax.dot_general(o_w[l, at, :], wide[...], (((1,), (1,)), ((), ())),
                                            preferred_element_type=F32)
                cores = cores.reshape(pair, nt, each, HD)
                to = pl.ds(pl.multiple_of(j * pair * each, pair * each), pair * each)
                for t in range(nt):
                    c_out[unit, t % 2, t // 2, to, :] = cores[:, t].reshape(pair * each, HD).astype(BF16)
                return 0

            lax.fori_loop(0, heads // pair, body, 0)
            if unit == last:
                second(unit - 1)
                d_copies = [pltpu.make_async_remote_copy(
                    src_ref=c_out.at[unit, lax.rem(t_to[d], 2), t_to[d] // 2],
                    dst_ref=c_dir.at[d], send_sem=d_send.at[d], recv_sem=d_recv.at[d],
                    device_id={"tile": t_to[d]}, device_id_type=MESH) for d in range(1, nt)]
                for copy in d_copies:
                    copy.start()
                continue
            m_copies.append(pltpu.make_async_remote_copy(
                src_ref=c_out.at[unit, other], dst_ref=c_mid.at[unit],
                send_sem=m_send.at[unit], recv_sem=m_recv.at[unit],
                device_id={"tile": mate}, device_id_type=MESH))
            m_copies[unit].start()
            if unit > 0:
                second(unit - 1)

    for kind in range(2):
        for l in range(layers):
            unit = kind * layers + l
            total = c_out[unit, parity, place].astype(F32)
            if unit == last:
                for d in range(1, nt):
                    d_copies[d - 1].wait_recv()
                    total += c_dir[d].astype(F32)
            else:
                total += c_mid[unit, place].astype(F32)
                for d in range(1, half):
                    c_copies[unit][d - 1].wait_recv()
                    total += c_in[unit, d].astype(F32)
            out_ref[1 - kind, l] = total.reshape(heads, each, HD)
    for copies in [e_across, e_beside, u_across, u_beside, m_copies, d_copies] + rs_copies + ag_copies + c_copies:
        for copy in copies:
            copy.wait_send()


def local(nv, nt, embed, unembed, q_weight, k_weight, v_weight, o_weight, offsets):
    layers, depth, width = q_weight.shape
    heads, rows, each = width // HD, nv * SLAB_DEV, HD // nt
    chunk, units = rows // nt, 2 * layers
    out = jax.ShapeDtypeStruct((2, layers, heads, each, HD), F32)
    anywhere = pl.BlockSpec(memory_space=pl.ANY)
    vmem, dma = pltpu.VMEM, pltpu.SemaphoreType.DMA
    cores = pl.pallas_call(
        functools.partial(kernel, nv, nt, layers, heads),
        out_shape=out,
        in_specs=[pl.BlockSpec(memory_space=pltpu.SMEM)] + [anywhere] * 6,
        out_specs=pl.BlockSpec(memory_space=pltpu.VMEM),
        scratch_shapes=[
            vmem(embed.shape, BF16), vmem(embed.shape, BF16),
            vmem((rows, depth), BF16), vmem((rows, depth), BF16),
            vmem((layers, depth, width), BF16), vmem((layers, width, depth), BF16),
            vmem((layers, depth, 2 * HD), BF16),
            vmem((2, nt, chunk, HD * layers), BF16), vmem((2, nt, chunk, HD * layers), BF16),
            vmem((2, nt, chunk, HD * layers), BF16),
            vmem((HD, depth), BF16),
            vmem((units, 2, nt // 2, heads * each, HD), BF16),
            vmem((units, nt // 2, heads * each, HD), BF16),
            vmem((units, nt // 2, heads * each, HD), BF16),
            vmem((units, nt // 2, heads * each, HD), BF16),
            vmem((nt, heads * each, HD), BF16),
            dma((2,)), dma((4 * layers,)), dma((nv,)), dma((nv,)), dma((nv,)), dma((nv,)),
            dma((2, nt)), dma((2, nt)), dma((2, nt)), dma((2, nt)),
            dma((units,)), dma((units,)), dma((units, nt // 2)), dma((units, nt // 2)),
            dma((nt,)), dma((nt,)),
        ],
        compiler_params=pltpu.CompilerParams(
            collective_id=0, has_side_effects=True, vmem_limit_bytes=61 * 2**20),
    )(offsets, embed, unembed, q_weight, k_weight, v_weight, o_weight)
    scale = 1.0 / math.sqrt(rows)
    return cores[0] * scale, cores[1] * scale


def solution(mesh):
    return jax.shard_map(
        functools.partial(local, mesh.shape["vocab"], mesh.shape["tile"]),
        mesh=mesh,
        in_specs=(
            P("vocab", "tile"),
            P("vocab", "tile"),
            P(None, "tile", "vocab"),
            P(None, "tile", None),
            P(None, "tile", None),
            P(None, "vocab", "tile"),
            P("grp"),
        ),
        out_specs=(P("grp", "vocab", "tile", None), P("grp", "vocab", "tile", None)),
        check_vma=False,
    )
```

```python
import functools
import math

import jax
import jax.numpy as jnp
from jax import lax
from jax.experimental import pallas as pl
from jax.experimental.pallas import tpu as pltpu
from jax.sharding import PartitionSpec as P

HD = 128
GROUP = 8
SLAB_DEV = 64
MESH = pl.DeviceIdType.MESH
BF16, F32 = jnp.bfloat16, jnp.float32


def kernel(nv, nt, layers, heads, off_ref, e_hbm, u_hbm, q_hbm, k_hbm, v_hbm, o_hbm,
           out_ref, e_raw, u_raw, e_all, u_all, q_w, o_w, kv_w, part, rs_in, kv_all,
           wide, c_out, c_mid, c_sum, c_in, raw_sem, w_sem, e_send, e_recv, u_send, u_recv,
           rs_send, rs_recv, ag_send, ag_recv, m_send, m_recv, c_send, c_recv):
    vme, tme = lax.axis_index("vocab"), lax.axis_index("tile")
    chips, half = nv // 2, nt // 2
    core = lax.rem(vme, 2)
    sibling = vme + 1 - 2 * core
    chip_to = [lax.rem(vme + 2 * d, nv) for d in range(chips)]
    parity, place = lax.rem(tme, 2), tme // 2
    other = 1 - parity
    mate = tme + 1 - 2 * parity
    place_to = [lax.rem(place + d, half) for d in range(half)]
    t_to = [lax.rem(tme + d, nt) for d in range(nt)]
    t_from = [lax.rem(tme + nt - d, nt) for d in range(nt)]
    depth = e_raw.shape[1]
    rows = nv * SLAB_DEV
    chunk = rows // nt
    each = HD // nt

    barrier = pltpu.get_barrier_semaphore()
    for v in [sibling] + chip_to[1:]:
        pl.semaphore_signal(barrier, inc=1, device_id={"vocab": v}, device_id_type=MESH)
    for d in range(1, nt):
        pl.semaphore_signal(barrier, inc=1, device_id={"tile": t_to[d]}, device_id_type=MESH)

    raw = [pltpu.make_async_copy(e_hbm, e_raw, raw_sem.at[0]),
           pltpu.make_async_copy(u_hbm, u_raw, raw_sem.at[1])]
    for copy in raw:
        copy.start()
    start = pl.multiple_of(vme * heads // GROUP * HD, HD)
    kv_loads = []
    for l in range(layers):
        for kind, src in enumerate((k_hbm, v_hbm)):
            kv_loads.append(pltpu.make_async_copy(
                src.at[l, :, pl.ds(start, HD)],
                kv_w.at[l, :, pl.ds(kind * HD, HD)], w_sem.at[2 * l + kind]))
    big_loads = []
    for kind, (src, dst) in enumerate(((q_hbm, q_w), (o_hbm, o_w))):
        for l in range(layers):
            big_loads.append(pltpu.make_async_copy(
                src.at[l], dst.at[l], w_sem.at[2 * layers + kind * layers + l]))

    for copy in kv_loads:
        copy.start()

    off = off_ref[0]
    row = lax.broadcasted_iota(jnp.int32, (SLAB_DEV, e_raw.shape[0]), 0)
    col = lax.broadcasted_iota(jnp.int32, (SLAB_DEV, e_raw.shape[0]), 1)
    pick = jnp.where(col == row + off, 1.0, 0.0).astype(BF16)
    raw[0].wait()
    e_all[:SLAB_DEV] = jnp.dot(pick, e_raw[...], preferred_element_type=F32).astype(BF16)

    pl.semaphore_wait(barrier, chips + nt - 1)

    def to_vocab(buf, src, dst, v, send, recv):
        return pltpu.make_async_remote_copy(
            src_ref=buf.at[pl.ds(src * SLAB_DEV, SLAB_DEV)],
            dst_ref=buf.at[pl.ds(dst * SLAB_DEV, SLAB_DEV)],
            send_sem=send.at[dst], recv_sem=recv.at[dst],
            device_id={"vocab": v}, device_id_type=MESH)

    def gather(buf, send, recv):
        across = [to_vocab(buf, 0, 2 * d, chip_to[d], send, recv) for d in range(1, chips)]
        beside = [to_vocab(buf, 2 * d, 2 * d + 1, sibling, send, recv) for d in range(chips)]
        return across, beside

    def forward(across, beside):
        for d in range(1, chips):
            across[d - 1].wait_recv()
            beside[d].start()

    e_across, e_beside = gather(e_all, e_send, e_recv)
    u_across, u_beside = gather(u_all, u_send, u_recv)
    for copy in e_across + e_beside[:1] + big_loads:
        copy.start()
    raw[1].wait()
    u_all[:SLAB_DEV] = jnp.dot(pick, u_raw[...], preferred_element_type=F32).astype(BF16)

    for copy in kv_loads:
        copy.wait()
    forward(e_across, e_beside)
    for copy in u_across + u_beside[:1]:
        copy.start()
    for copy in e_beside:
        copy.wait_recv()

    rs_copies, ag_copies = [], []
    for kind in range(2):
        for l in range(layers):
            got = jnp.dot(e_all[...], kv_w[l, :, kind * HD:(kind + 1) * HD],
                          preferred_element_type=F32).astype(BF16)
            for t in range(nt):
                part[kind, t, :, HD * l:HD * (l + 1)] = got[t * chunk:(t + 1) * chunk]
        rs_copies.append([pltpu.make_async_remote_copy(
            src_ref=part.at[kind, t_to[d]], dst_ref=rs_in.at[kind, d],
            send_sem=rs_send.at[kind, d], recv_sem=rs_recv.at[kind, d],
            device_id={"tile": t_to[d]}, device_id_type=MESH) for d in range(1, nt)])
        for copy in rs_copies[kind]:
            copy.start()
    for kind in range(2):
        total = part[kind, tme].astype(F32)
        for d in range(1, nt):
            rs_copies[kind][d - 1].wait_recv()
            total += rs_in[kind, d].astype(F32)
        kv_all[kind, tme] = total.astype(BF16)
        ag_copies.append([pltpu.make_async_remote_copy(
            src_ref=kv_all.at[kind, tme], dst_ref=kv_all.at[kind, tme],
            send_sem=ag_send.at[kind, d], recv_sem=ag_recv.at[kind, d],
            device_id={"tile": t_to[d]}, device_id_type=MESH) for d in range(1, nt)])
        for copy in ag_copies[kind]:
            copy.start()
    forward(u_across, u_beside)

    step = min(2 * HD, heads * HD)
    pair = step // HD
    m_copies, c_copies = [], []

    def second(unit):
        m_copies[unit].wait_recv()
        copies = []
        for d in range(1, half):
            k = place_to[d]
            c_sum[unit, d] = (c_out[unit, parity, k].astype(F32)
                              + c_mid[unit, k].astype(F32)).astype(BF16)
            copies.append(pltpu.make_async_remote_copy(
                src_ref=c_sum.at[unit, d], dst_ref=c_in.at[unit, d],
                send_sem=c_send.at[unit, d], recv_sem=c_recv.at[unit, d],
                device_id={"tile": 2 * k + parity}, device_id_type=MESH))
            copies[-1].start()
        c_copies.append(copies)

    for kind in range(2):
        slab = e_all if kind == 0 else u_all
        for d in range(1, nt):
            at = kv_all.at[kind, t_from[d]]
            pltpu.make_async_remote_copy(
                src_ref=at, dst_ref=at, send_sem=ag_send.at[kind, d],
                recv_sem=ag_recv.at[kind, d], device_id={"tile": t_to[d]},
                device_id_type=MESH).wait_recv()
        if kind == 1:
            for copy in u_beside:
                copy.wait_recv()
        for l in range(layers):
            unit = kind * layers + l
            side = kv_all[kind, :, :, HD * l:HD * (l + 1)].reshape(rows, HD)
            wide[...] = lax.dot_general(side, slab[...], (((0,), (0,)), ((), ())),
                                        preferred_element_type=F32).astype(BF16)
            big_loads[unit].wait()

            def body(j, _):
                at = pl.ds(pl.multiple_of(j * step, step), step)
                if kind == 0:
                    cores = jnp.dot(wide[...], q_w[l, :, at], preferred_element_type=F32).T
                else:
                    cores = lax.dot_general(o_w[l, at, :], wide[...], (((1,), (1,)), ((), ())),
                                            preferred_element_type=F32)
                cores = cores.reshape(pair, nt, each, HD)
                to = pl.ds(pl.multiple_of(j * pair * each, pair * each), pair * each)
                for t in range(nt):
                    c_out[unit, t % 2, t // 2, to, :] = cores[:, t].reshape(pair * each, HD).astype(BF16)
                return 0

            lax.fori_loop(0, heads // pair, body, 0)
            m_copies.append(pltpu.make_async_remote_copy(
                src_ref=c_out.at[unit, other], dst_ref=c_mid.at[unit],
                send_sem=m_send.at[unit], recv_sem=m_recv.at[unit],
                device_id={"tile": mate}, device_id_type=MESH))
            m_copies[unit].start()
            if unit > 0:
                second(unit - 1)
    second(2 * layers - 1)

    for kind in range(2):
        for l in range(layers):
            unit = kind * layers + l
            total = c_out[unit, parity, place].astype(F32) + c_mid[unit, place].astype(F32)
            for d in range(1, half):
                c_copies[unit][d - 1].wait_recv()
                total += c_in[unit, d].astype(F32)
            out_ref[1 - kind, l] = total.reshape(heads, each, HD)
    for copies in [e_across, e_beside, u_across, u_beside, m_copies] + rs_copies + ag_copies + c_copies:
        for copy in copies:
            copy.wait_send()


def local(nv, nt, embed, unembed, q_weight, k_weight, v_weight, o_weight, offsets):
    layers, depth, width = q_weight.shape
    heads, rows, each = width // HD, nv * SLAB_DEV, HD // nt
    chunk, units = rows // nt, 2 * layers
    out = jax.ShapeDtypeStruct((2, layers, heads, each, HD), F32)
    anywhere = pl.BlockSpec(memory_space=pl.ANY)
    vmem, dma = pltpu.VMEM, pltpu.SemaphoreType.DMA
    cores = pl.pallas_call(
        functools.partial(kernel, nv, nt, layers, heads),
        out_shape=out,
        in_specs=[pl.BlockSpec(memory_space=pltpu.SMEM)] + [anywhere] * 6,
        out_specs=pl.BlockSpec(memory_space=pltpu.VMEM),
        scratch_shapes=[
            vmem(embed.shape, BF16), vmem(embed.shape, BF16),
            vmem((rows, depth), BF16), vmem((rows, depth), BF16),
            vmem((layers, depth, width), BF16), vmem((layers, width, depth), BF16),
            vmem((layers, depth, 2 * HD), BF16),
            vmem((2, nt, chunk, HD * layers), BF16), vmem((2, nt, chunk, HD * layers), BF16),
            vmem((2, nt, chunk, HD * layers), BF16),
            vmem((HD, depth), BF16),
            vmem((units, 2, nt // 2, heads * each, HD), BF16),
            vmem((units, nt // 2, heads * each, HD), BF16),
            vmem((units, nt // 2, heads * each, HD), BF16),
            vmem((units, nt // 2, heads * each, HD), BF16),
            dma((2,)), dma((4 * layers,)), dma((nv,)), dma((nv,)), dma((nv,)), dma((nv,)),
            dma((2, nt)), dma((2, nt)), dma((2, nt)), dma((2, nt)),
            dma((units,)), dma((units,)), dma((units, nt // 2)), dma((units, nt // 2)),
        ],
        compiler_params=pltpu.CompilerParams(
            collective_id=0, has_side_effects=True, vmem_limit_bytes=61 * 2**20),
    )(offsets, embed, unembed, q_weight, k_weight, v_weight, o_weight)
    scale = 1.0 / math.sqrt(rows)
    return cores[0] * scale, cores[1] * scale


def solution(mesh):
    return jax.shard_map(
        functools.partial(local, mesh.shape["vocab"], mesh.shape["tile"]),
        mesh=mesh,
        in_specs=(
            P("vocab", "tile"),
            P("vocab", "tile"),
            P(None, "tile", "vocab"),
            P(None, "tile", None),
            P(None, "tile", None),
            P(None, "vocab", "tile"),
            P("grp"),
        ),
        out_specs=(P("grp", "vocab", "tile", None), P("grp", "vocab", "tile", None)),
        check_vma=False,
    )
```
